512 devices in a mesh: depth: 4 (over x), row: 8 (over z_lo), col: 16 (over y, z_hi, core).
Axes of the slice: x: 4, y: 4, z: 16 (z_hi: 2, z_lo: 8; z = z_hi * 8 + z_lo), core: 2. Of those that a mesh axis runs over, the one named last changes fastest.
Arguments:
- inputs: bfloat16 [1024, 16384], P('row', 'col'), may hold values from -6 to 6
- out_grad: bfloat16 [1024, 32768], P('col', ('depth', 'row')), may hold values from -6 to 6
- weight: bfloat16 [16384, 32768], P('col', ('depth', 'row')), may hold values from -0.046875 to 0.046875
Outputs:
- input_grad: bfloat16 [1024, 16384], P(('depth', 'row'), 'col')
- weight_grad: bfloat16 [16384, 32768], P('col', ('depth', 'row'))
The draws below stay inside these ranges and needn't reach their ends.
All inputs are finite; a program needn't handle non-finite values.
Results may differ from the reference program's by a relative error of at most 0.0011.
Values may be sent and summed in bfloat16 or wider, within the bound.
A program may use at most 64 MiB of HBM per device.

```python
import jax
import jax.numpy as jnp

D = 16384
FF = 32768
TOK = 1024


def spiked(values, own_key, source, target, shards_of, factor):
    def block_of(dim):
        return (jnp.arange(values.shape[dim]) // (values.shape[dim] // shards_of)).reshape((-1,) + (1,) * (values.ndim - 1 - dim))

    near = jax.random.permutation(own_key, shards_of)[block_of(target)]
    far = (block_of(target) + shards_of // 2) % shards_of
    return jnp.where((block_of(source) == near) | (block_of(source) == far), factor * values, values)


def levels(key, shape, shards, smallest, high):
    def one(dim, blocks):
        heights = jax.random.uniform(jax.random.fold_in(jax.random.fold_in(key, 6), dim), (blocks,), jnp.float32, smallest / len(shards), high / len(shards))
        return jnp.repeat(jnp.exp(heights), shape[dim] // blocks).reshape((-1,) + (1,) * (len(shape) - dim - 1))

    loudness = one(*shards[0])
    for cut in shards[1:]:
        loudness = loudness * one(*cut)
    return loudness


def normal_values(rng, dims, width, reach, cuts=(), held_as=jnp.bfloat16):
    array = jax.random.normal(rng, dims, jnp.float32) * width
    if len(cuts) > 0:
        array = levels(rng, dims, cuts, -0.22, 0.18) * array
    return jnp.clip(array, min=-reach, max=reach).astype(held_as)


def noise_with(own_key, dims, deviation, bound, shards, heavy, held_as=jnp.bfloat16):
    result = deviation * jax.random.normal(own_key, dims, jnp.float32)
    if shards:
        result = result * levels(own_key, dims, shards, -0.22, 0.18)
    return jnp.clip(spiked(result, jax.random.fold_in(own_key, 3), *heavy), -bound, bound).astype(held_as)


def setup_inputs(seed: int = 0) -> dict:
    key_list = jax.random.split(jax.random.key(seed), 4)
    inputs = normal_values(key_list[0], (TOK, D), 1.0, 6.0, ((0, 8), (1, 16)))
    out_grad = noise_with(key_list[1], (TOK, FF), 1.0, 6.0, ((0, 16), (1, 32)), (1, 0, 32, 2.75))
    weight = normal_values(key_list[2], (D, FF), D ** -0.5, 0.046875, ((0, 16), (1, 32)))
    return dict(inputs=inputs, out_grad=out_grad, weight=weight)


def reference(inputs, out_grad, weight):
    input_grad = jnp.dot(out_grad, weight.T, preferred_element_type=jnp.float32).astype(jnp.bfloat16)
    summed = jnp.dot(inputs.T, out_grad, preferred_element_type=jnp.float32)
    weight_grad = (summed * (1.0 / TOK)).astype(jnp.bfloat16)
    return input_grad, weight_grad
```

```python
import jax
import jax.numpy as jnp
from jax import lax
from jax.experimental import pallas as pl
from jax.experimental.pallas import tpu as pltpu
from jax.sharding import PartitionSpec as P

MESH = pl.DeviceIdType.MESH
F32 = jnp.float32
BF16 = jnp.bfloat16
PEAK = 200.0


def encode(value, code_ref, scale_ref):
    size = jnp.abs(value)
    top = jnp.max(jnp.max(size, axis=0, keepdims=True), axis=1, keepdims=True)
    top = jnp.maximum(top, 1e-30)
    power = size * (PEAK / top)
    for _ in range(4):
        power = power * power
    code_ref[...] = jnp.where(value < 0, -power, power).astype(BF16)
    scale_ref[...] = jnp.broadcast_to(top * (1.0 / PEAK), scale_ref.shape)


def decode(code_ref, scale_ref):
    code = code_ref[...].astype(F32)
    size = jnp.exp2(jnp.log2(jnp.abs(code)) * 0.0625)
    size = jnp.where(code == 0, 0.0, size) * scale_ref[0:1, 0:1]
    return jnp.where(code < 0, -size, size)


def kernel(
    x_hbm, g_hbm, w_hbm, ig_ref, dw_hbm,
    w, g, xs, acc, dw, part, own, fin,
    xc_s, xc_r, xk_s, xk_r,
    zc_s, zc_r, zk_s, zk_r,
    bc_s, bc_r, bk_s, bk_r,
    local, out_sem,
    gz_s, gz_r, gy_s, gy_r, gk_s, gk_r,
    cx_s, cx_r, kx_s, kx_r,
    cz_s, cz_r, kz_s, kz_r,
    cb_s, cb_r,
    xz_s, xz_r, xx_s, xx_r,
):
    x = lax.axis_index("depth")
    zl = lax.axis_index("row")
    col = lax.axis_index("col")
    y, zh, core = col // 4, (col // 2) % 2, col % 2
    quad, pos = zl // 4, zl % 4

    def y_dev(o):
        return (x, zl, lax.rem(y + o, 4) * 4 + zh * 2 + core)

    def x_dev(o):
        return (lax.rem(x + o, 4), zl, col)

    def q_dev(o):
        return (x, quad * 4 + lax.rem(pos + o, 4), col)

    z8_dev = (x, zl, y * 4 + (1 - zh) * 2 + core)
    sib_dev = (x, zl, y * 4 + zh * 2 + (1 - core))
    z4_dev = (x, (1 - quad) * 4 + pos, col)

    def remote(src, dst, send, recv, device):
        return pltpu.make_async_remote_copy(
            src_ref=src, dst_ref=dst, send_sem=send, recv_sem=recv, device_id=device, device_id_type=MESH
        )

    def g_rows(yy, zz, kk):
        return pl.ds(pl.multiple_of(yy * 256 + zz * 128 + kk * 64, 64), 64)

    load_w = pltpu.make_async_copy(w_hbm, w, local.at[0])
    load_g = pltpu.make_async_copy(g_hbm, g.at[g_rows(y, zh, core)], local.at[1])
    load_w.start()
    load_g.start()
    loads_x = []
    for q in range(4):
        c = pltpu.make_async_copy(x_hbm.at[pl.ds(q * 32, 32)], xs.at[zl, q], local.at[2 + q])
        c.start()
        loads_x.append(c)

    barrier = pltpu.get_barrier_semaphore()
    partners = [z8_dev, sib_dev, z4_dev]
    partners += [f(o) for f in (y_dev, x_dev, q_dev) for o in (1, 2, 3)]
    for device in partners:
        pl.semaphore_signal(barrier, inc=1, device_id=device, device_id_type=MESH)
    pl.semaphore_wait(barrier, len(partners))

    pending = []

    gz = remote(g_hbm, g.at[g_rows(y, zh, core)], gz_s, gz_r, z8_dev)
    gz.start()
    pending.append(gz)

    def spread(ph, zz, src):
        for o in (1, 3, 2):
            c = remote(src, g.at[g_rows(y, zz, core)], gy_s.at[ph, o - 1], gy_r.at[ph, o - 1], y_dev(o))
            c.start()
            pending.append(c)
        c = remote(src, g.at[g_rows(y, zz, core)], gk_s.at[ph, 0], gk_r.at[ph, 0], sib_dev)
        c.start()
        pending.append(c)

    def forward(ph, zz, o):
        rows = g_rows(lax.rem(y + 4 - o, 4), zz, core)
        remote(g.at[rows], g.at[rows], gy_s.at[ph, o - 1], gy_r.at[ph, o - 1], y_dev(o)).wait_recv()
        c = remote(g.at[rows], g.at[rows], gk_s.at[ph, o], gk_r.at[ph, o], sib_dev)
        c.start()
        pending.append(c)

    def from_sibling(ph, zz, o):
        rows = g_rows(lax.rem(y + 4 - o, 4), zz, 1 - core)
        remote(g.at[rows], g.at[rows], gk_s.at[ph, o], gk_r.at[ph, o], sib_dev).wait_recv()

    def partial(ph, zz, o):
        target = lax.rem(y + 4 - o, 4)
        rows = pl.ds(pl.multiple_of(target * 256 + zz * 128, 128), 128)

        @pl.loop(0, 4)
        def _(t):
            cols = pl.ds(pl.multiple_of(t * 256, 256), 256)
            part[:, cols] = lax.dot_general(
                g[rows, :], w[cols, :], (((1,), (1,)), ((), ())), preferred_element_type=F32
            )

        @pl.when(target == x)
        def _():
            own[ph] = part[...]

        @pl.when(target != x)
        def _():
            slot = lax.rem(x - target + 4, 4) - 1
            encode(part[...], xc_s.at[ph, slot], xk_s.at[ph, slot])
            device = (target, zl, col)
            remote(xc_s.at[ph, slot], xc_r.at[ph, slot], cx_s.at[ph, slot], cx_r.at[ph, slot], device).start()
            remote(xk_s.at[ph, slot], xk_r.at[ph, slot], kx_s.at[ph, slot], kx_r.at[ph, slot], device).start()

    def sum_x(ph):
        for s in range(3):
            remote(xc_s.at[ph, s], xc_r.at[ph, s], cx_s.at[ph, s], cx_r.at[ph, s], x_dev(1)).wait_recv()
            remote(xk_s.at[ph, s], xk_r.at[ph, s], kx_s.at[ph, s], kx_r.at[ph, s], x_dev(1)).wait_recv()

        @pl.loop(0, 4)
        def _(b):
            rows = pl.ds(pl.multiple_of(b * 32, 32), 32)
            total = own[ph, rows, :]
            for s in range(3):
                total = total + decode(xc_r.at[ph, s, rows], xk_r.at[ph, s])
            own[ph, rows, :] = total

        for o in (1, 2, 3):
            rows = pl.ds(pl.multiple_of(lax.rem(pos + o, 4) * 32, 32), 32)
            s = o - 1
            encode(own[ph, rows, :], zc_s.at[ph, s], zk_s.at[ph, s])
            c = remote(zc_s.at[ph, s], zc_r.at[ph, s], cz_s.at[ph, s], cz_r.at[ph, s], q_dev(o))
            c.start()
            pending.append(c)
            c = remote(zk_s.at[ph, s], zk_r.at[ph, s], kz_s.at[ph, s], kz_r.at[ph, s], q_dev(o))
            c.start()
            pending.append(c)

    def cross(i):
        code = remote(bc_s, bc_r, cb_s.at[0], cb_r.at[0], z4_dev)
        scale = remote(bk_s, bk_r, cb_s.at[1], cb_r.at[1], z4_dev)
        return code, scale

    def sum_quad(ph, zz):
        total = own[ph, pl.ds(pl.multiple_of(pos * 32, 32), 32), :]
        for s in range(3):
            remote(zc_s.at[ph, s], zc_r.at[ph, s], cz_s.at[ph, s], cz_r.at[ph, s], q_dev(1)).wait_recv()
            remote(zk_s.at[ph, s], zk_r.at[ph, s], kz_s.at[ph, s], kz_r.at[ph, s], q_dev(1)).wait_recv()
            total = total + decode(zc_r.at[ph, s], zk_r.at[ph, s])
        fin[ph] = total

        @pl.when(zz != quad)
        def _():
            encode(fin[ph], bc_s, bk_s)
            for c in cross(0):
                c.start()

    spread(0, zh, g_hbm)
    load_g.wait()
    load_w.wait()
    from_sibling(0, zh, 0)
    partial(0, zh, 0)
    forward(0, zh, 1)
    forward(0, zh, 3)
    from_sibling(0, zh, 1)
    partial(0, zh, 1)
    from_sibling(0, zh, 3)
    partial(0, zh, 3)
    forward(0, zh, 2)
    from_sibling(0, zh, 2)
    partial(0, zh, 2)

    far = 1 - zh
    far_rows = g_rows(y, far, core)
    remote(g.at[far_rows], g.at[far_rows], gz_s, gz_r, z8_dev).wait_recv()
    spread(1, far, g.at[far_rows])

    mine = x_hbm.at[pl.ds(pl.multiple_of(x * 32, 32), 32)]
    for o in (1, 2, 3):
        c = remote(mine, xs.at[zl, x], xz_s.at[o - 1], xz_r.at[o - 1], q_dev(o))
        c.start()
        pending.append(c)
    c = remote(mine, xs.at[zl, x], xz_s.at[3], xz_r.at[3], z4_dev)
    c.start()
    pending.append(c)

    from_sibling(1, far, 0)
    partial(1, far, 0)
    forward(1, far, 1)
    forward(1, far, 3)
    from_sibling(1, far, 1)
    partial(1, far, 1)
    from_sibling(1, far, 3)
    partial(1, far, 3)
    forward(1, far, 2)
    from_sibling(1, far, 2)
    partial(1, far, 2)

    sum_x(0)

    zo = (1 - quad) * 4 + pos
    remote(xs.at[zo, x], xs.at[zo, x], xz_s.at[3], xz_r.at[3], z4_dev).wait_recv()
    for o in (1, 2, 3):
        c = remote(xs.at[zo, x], xs.at[zo, x], xz_s.at[3 + o], xz_r.at[3 + o], q_dev(o))
        c.start()
        pending.append(c)

    sum_quad(0, zh)
    sum_x(1)

    for o in (1, 2, 3):
        zs = quad * 4 + lax.rem(pos + 4 - o, 4)
        remote(xs.at[zs, x], xs.at[zs, x], xz_s.at[o - 1], xz_r.at[o - 1], q_dev(1)).wait_recv()
        for p in (1, 3, 2):
            c = remote(xs.at[zs, x], xs.at[zs, x], xx_s.at[p - 1, o - 1], xx_r.at[p - 1, o - 1], x_dev(p))
            c.start()
            pending.append(c)
    for o in (1, 2, 3):
        zs = (1 - quad) * 4 + lax.rem(pos + 4 - o, 4)
        remote(xs.at[zs, x], xs.at[zs, x], xz_s.at[3 + o], xz_r.at[3 + o], q_dev(1)).wait_recv()
    others = pl.ds(pl.multiple_of((1 - quad) * 4, 4), 4)
    for p in (1, 3, 2):
        c = remote(xs.at[others, x], xs.at[others, x], xx_s.at[p - 1, 3], xx_r.at[p - 1, 3], x_dev(p))
        c.start()
        pending.append(c)

    sum_quad(1, far)

    for c in loads_x:
        c.wait()
    for p in (1, 2, 3):
        xo = lax.rem(x + 4 - p, 4)
        for o in (1, 2, 3):
            zs = quad * 4 + lax.rem(pos + 4 - o, 4)
            remote(xs.at[zs, xo], xs.at[zs, xo], xx_s.at[p - 1, o - 1], xx_r.at[p - 1, o - 1], x_dev(p)).wait_recv()

    def product(qd, t):
        rows = pl.ds(pl.multiple_of(qd * 4, 4), 4)
        cols = pl.ds(pl.multiple_of(t * 256, 256), 256)
        lhs = xs[rows, :, :, cols].reshape(512, 256)
        rhs = g[pl.ds(pl.multiple_of(qd * 512, 512), 512), :]
        return lax.dot_general(lhs, rhs, (((0,), (0,)), ((), ())), preferred_element_type=F32)

    @pl.loop(0, 4)
    def _(t):
        acc[pl.ds(pl.multiple_of(t * 256, 256), 256), :] = product(quad, t)

    for c in cross(0):
        c.wait_recv()
    mine_ph = jnp.where(quad == zh, 0, 1)
    ig_ref[...] = (fin[mine_ph] + decode(bc_r, bk_r)).astype(BF16)

    for p in (1, 2, 3):
        xo = lax.rem(x + 4 - p, 4)
        remote(xs.at[others, xo], xs.at[others, xo], xx_s.at[p - 1, 3], xx_r.at[p - 1, 3], x_dev(p)).wait_recv()

    @pl.loop(0, 4)
    def _(t):
        rows = pl.ds(pl.multiple_of(t * 256, 256), 256)
        dw[rows, :] = ((acc[rows, :] + product(1 - quad, t)) * (1.0 / 1024)).astype(BF16)
        pltpu.make_async_copy(dw.at[rows], dw_hbm.at[rows], out_sem.at[t]).start()

    for c in pending:
        c.wait_send()
    for c in cross(0):
        c.wait_send()
    for ph in range(2):
        for s in range(3):
            remote(xc_s.at[ph, s], xc_r.at[ph, s], cx_s.at[ph, s], cx_r.at[ph, s], x_dev(1)).wait_send()
            remote(xk_s.at[ph, s], xk_r.at[ph, s], kx_s.at[ph, s], kx_r.at[ph, s], x_dev(1)).wait_send()

    @pl.loop(0, 4)
    def _(t):
        rows = pl.ds(pl.multiple_of(t * 256, 256), 256)
        pltpu.make_async_copy(dw.at[rows], dw_hbm.at[rows], out_sem.at[t]).wait()


def per_device(inputs, out_grad, weight):
    dma = pltpu.SemaphoreType.DMA
    vmem = pltpu.VMEM
    return pl.pallas_call(
        kernel,
        out_shape=(
            jax.ShapeDtypeStruct((32, 1024), BF16),
            jax.ShapeDtypeStruct((1024, 1024), BF16),
        ),
        in_specs=[pl.BlockSpec(memory_space=pl.ANY)] * 3,
        out_specs=(pl.BlockSpec(memory_space=vmem), pl.BlockSpec(memory_space=pl.ANY)),
        scratch_shapes=[
            vmem((1024, 1024), BF16),
            vmem((1024, 1024), BF16),
            vmem((8, 4, 32, 1024), BF16),
            vmem((1024, 1024), F32),
            vmem((1024, 1024), BF16),
            vmem((128, 1024), F32),
            vmem((2, 128, 1024), F32),
            vmem((2, 32, 1024), F32),
            vmem((2, 3, 128, 1024), BF16),
            vmem((2, 3, 128, 1024), BF16),
            vmem((2, 3, 8, 128), F32),
            vmem((2, 3, 8, 128), F32),
            vmem((2, 3, 32, 1024), BF16),
            vmem((2, 3, 32, 1024), BF16),
            vmem((2, 3, 8, 128), F32),
            vmem((2, 3, 8, 128), F32),
            vmem((32, 1024), BF16),
            vmem((32, 1024), BF16),
            vmem((8, 128), F32),
            vmem((8, 128), F32),
            dma((6,)),
            dma((4,)),
            dma,
            dma,
            dma((2, 3)),
            dma((2, 3)),
            dma((2, 4)),
            dma((2, 4)),
            dma((2, 3)),
            dma((2, 3)),
            dma((2, 3)),
            dma((2, 3)),
            dma((2, 3)),
            dma((2, 3)),
            dma((2, 3)),
            dma((2, 3)),
            dma((2,)),
            dma((2,)),
            dma((7,)),
            dma((7,)),
            dma((3, 4)),
            dma((3, 4)),
        ],
        compiler_params=pltpu.CompilerParams(
            collective_id=0, has_side_effects=True, vmem_limit_bytes=48 * 1024 * 1024
        ),
        cost_estimate=pl.CostEstimate(flops=4 * 1024**3, bytes_accessed=7 * 1024**2, transcendentals=0),
        name="grads",
    )(inputs, out_grad, weight)


def solution(mesh):
    return jax.shard_map(
        per_device,
        mesh=mesh,
        in_specs=(P("row", "col"), P("col", ("depth", "row")), P("col", ("depth", "row"))),
        out_specs=(P(("depth", "row"), "col"), P("col", ("depth", "row"))),
        check_vma=False,
    )
```

```python
import jax
import jax.numpy as jnp
from jax import lax
from jax.experimental import pallas as pl
from jax.experimental.pallas import tpu as pltpu
from jax.sharding import PartitionSpec as P

MESH = pl.DeviceIdType.MESH
F32 = jnp.float32
BF16 = jnp.bfloat16
PEAK = 200.0


def encode(value, code_ref, scale_ref):
    size = jnp.abs(value)
    top = jnp.max(jnp.max(size, axis=0, keepdims=True), axis=1, keepdims=True)
    top = jnp.maximum(top, 1e-30)
    power = size * (PEAK / top)
    for _ in range(4):
        power = power * power
    code_ref[...] = jnp.where(value < 0, -power, power).astype(BF16)
    scale_ref[...] = jnp.broadcast_to(top * (1.0 / PEAK), scale_ref.shape)


def decode(code_ref, scale_ref):
    code = code_ref[...].astype(F32)
    size = jnp.exp2(jnp.log2(jnp.abs(code)) * 0.0625)
    size = jnp.where(code == 0, 0.0, size) * scale_ref[0:1, 0:1]
    return jnp.where(code < 0, -size, size)


def kernel(
    x_hbm, g_hbm, w_hbm, ig_ref, dw_hbm,
    w, g, xs, acc, dw, part, own, fin,
    xc_s, xc_r, xk_s, xk_r,
    zc_s, zc_r, zk_s, zk_r,
    bc_s, bc_r, bk_s, bk_r,
    local, out_sem, near_in, far_in,
    gz_s, gz_r, gy_s, gy_r, gk_s, gk_r,
    cx_s, cx_r, kx_s, kx_r,
    cz_s, cz_r, kz_s, kz_r,
    cb_s, cb_r,
    xz_s, xz_r, xx_s, xx_r,
):
    x = lax.axis_index("depth")
    zl = lax.axis_index("row")
    col = lax.axis_index("col")
    y, zh, core = col // 4, (col // 2) % 2, col % 2
    quad, pos = zl // 4, zl % 4

    def y_dev(o):
        return (x, zl, lax.rem(y + o, 4) * 4 + zh * 2 + core)

    def x_dev(o):
        return (lax.rem(x + o, 4), zl, col)

    def q_dev(o):
        return (x, quad * 4 + lax.rem(pos + o, 4), col)

    z8_dev = (x, zl, y * 4 + (1 - zh) * 2 + core)
    sib_dev = (x, zl, y * 4 + zh * 2 + (1 - core))
    z4_dev = (x, (1 - quad) * 4 + pos, col)

    def remote(src, dst, send, recv, device):
        return pltpu.make_async_remote_copy(
            src_ref=src, dst_ref=dst, send_sem=send, recv_sem=recv, device_id=device, device_id_type=MESH
        )

    load_w = pltpu.make_async_copy(w_hbm, w, local.at[0])
    load_g = pltpu.make_async_copy(g_hbm, g.at[y, zh, core], local.at[1])
    load_w.start()
    load_g.start()
    loads_x = []
    for q in range(4):
        c = pltpu.make_async_copy(x_hbm.at[pl.ds(q * 32, 32)], xs.at[zl, q], local.at[2 + q])
        c.start()
        loads_x.append(c)

    def signal(semaphore, device):
        pl.semaphore_signal(semaphore, inc=1, device_id=device, device_id_type=MESH)

    barrier = pltpu.get_barrier_semaphore()
    for device in [sib_dev] + [f(o) for f in (y_dev, x_dev) for o in (1, 2, 3)]:
        signal(barrier, device)
    for o in (1, 2, 3):
        pl.when(pos + o < 4)(lambda o=o: signal(barrier, q_dev(o)))
    pl.when(quad == 0)(lambda: signal(barrier, z4_dev))
    pl.when(zh == 0)(lambda: signal(barrier, z8_dev))
    pl.semaphore_wait(barrier, 7 + pos + quad + zh)
    pl.when(zh == 1)(lambda: signal(far_in, z8_dev))
    for o in (1, 2, 3):
        pl.when(pos + o >= 4)(lambda o=o: signal(near_in, q_dev(o)))
    pl.when(quad == 1)(lambda: signal(near_in, z4_dev))

    pending = []

    far = 1 - zh
    to_far = [remote(g_hbm.at[pl.ds(32 * h, 32)], g.at[y, zh, core, pl.ds(32 * h, 32)], gz_s.at[h], gz_r.at[h], z8_dev) for h in (0, 1)]
    pending += to_far

    @pl.when(zh == 1)
    def _():
        for c in to_far:
            c.start()

    def chunk(yy, zz, kk, h):
        return g.at[yy, zz, kk, pl.ds(32 * h, 32)]

    def spread(ph, h, zz):
        src = chunk(y, zz, core, h)
        for o in (1, 3, 2):
            c = remote(src, src, gy_s.at[ph, h, o - 1], gy_r.at[ph, h, o - 1], y_dev(o))
            c.start()
            pending.append(c)
        c = remote(src, src, gk_s.at[ph, h, 0], gk_r.at[ph, h, 0], sib_dev)
        c.start()
        pending.append(c)

    def collect(ph, h, zz):
        for o in (1, 3, 2):
            block = chunk(lax.rem(y + 4 - o, 4), zz, core, h)
            remote(block, block, gy_s.at[ph, h, o - 1], gy_r.at[ph, h, o - 1], y_dev(o)).wait_recv()
            c = remote(block, block, gk_s.at[ph, h, o], gk_r.at[ph, h, o], sib_dev)
            c.start()
            pending.append(c)
        for o in (0, 1, 3, 2):
            block = chunk(lax.rem(y + 4 - o, 4), zz, 1 - core, h)
            remote(block, block, gk_s.at[ph, h, o], gk_r.at[ph, h, o], sib_dev).wait_recv()

    def partial(ph, h, zz):
        part[...] = lax.dot_general(
            g[:, zz, :, pl.ds(32 * h, 32), :].reshape(256, 1024),
            w[...],
            (((1,), (1,)), ((), ())),
            preferred_element_type=F32,
        )

        for o in (2, 1, 3):
            target = lax.rem(x + o, 4)
            rows = pl.ds(pl.multiple_of(target * 64, 64), 64)
            s = o - 1
            encode(part[rows, :], xc_s.at[ph, h, s], xk_s.at[ph, h, s])
            c = remote(xc_s.at[ph, h, s], xc_r.at[ph, h, s], cx_s.at[ph, h, s], cx_r.at[ph, h, s], x_dev(o))
            c.start()
            pending.append(c)
            c = remote(xk_s.at[ph, h, s], xk_r.at[ph, h, s], kx_s.at[ph, h, s], kx_r.at[ph, h, s], x_dev(o))
            c.start()
            pending.append(c)
        own[ph, h] = part[pl.ds(pl.multiple_of(x * 64, 64), 64), :]

    def to_quad(ph, slot, device):
        code = remote(zc_s.at[ph, slot], zc_r.at[ph, slot], cz_s.at[ph, slot], cz_r.at[ph, slot], device)
        scale = remote(zk_s.at[ph, slot], zk_r.at[ph, slot], kz_s.at[ph, slot], kz_r.at[ph, slot], device)
        return code, scale

    def sum_x(ph, h):
        for s in range(3):
            remote(xc_s.at[ph, h, s], xc_r.at[ph, h, s], cx_s.at[ph, h, s], cx_r.at[ph, h, s], x_dev(1)).wait_recv()
            remote(xk_s.at[ph, h, s], xk_r.at[ph, h, s], kx_s.at[ph, h, s], kx_r.at[ph, h, s], x_dev(1)).wait_recv()
        for k in (0, 1):
            rows = pl.ds(k * 32, 32)
            total = own[ph, h, rows, :]
            for s in range(3):
                total = total + decode(xc_r.at[ph, h, s, rows], xk_r.at[ph, h, s])
            own[ph, h, rows, :] = total
            there = 2 * k + h

            @pl.when(pos != there)
            def _():
                slot = lax.rem(there - pos + 4, 4) - 1
                encode(own[ph, h, rows, :], zc_s.at[ph, slot], zk_s.at[ph, slot])
                for c in to_quad(ph, slot, (x, quad * 4 + there, col)):
                    c.start()

    def cross():
        code = remote(bc_s, bc_r, cb_s.at[0], cb_r.at[0], z4_dev)
        scale = remote(bk_s, bk_r, cb_s.at[1], cb_r.at[1], z4_dev)
        return code, scale

    def sum_quad(ph, h, zz):
        @pl.when(lax.rem(pos, 2) == h)
        def _():
            total = own[ph, h, pl.ds(pl.multiple_of(pos // 2 * 32, 32), 32), :]
            for s in range(3):
                for c in to_quad(ph, s, q_dev(1)):
                    c.wait_recv()
                total = total + decode(zc_r.at[ph, s], zk_r.at[ph, s])
            fin[ph] = total

            @pl.when(zz != quad)
            def _():
                encode(fin[ph], bc_s, bk_s)
                for c in cross():
                    c.start()

    def near_spread():
        load_g.wait()
        for h in (0, 1):
            spread(0, h, zh)
        load_w.wait()

    def near_part(h):
        collect(0, h, zh)
        partial(0, h, zh)

    def far_send():
        @pl.when(zh == 0)
        def _():
            pl.semaphore_wait(far_in, 1)
            for c in to_far:
                c.start()

    def far_take(h):
        block = chunk(y, far, core, h)
        remote(block, block, gz_s.at[h], gz_r.at[h], z8_dev).wait_recv()
        spread(1, h, far)

    def far_part(h):
        collect(1, h, far)
        partial(1, h, far)

    mine = x_hbm.at[pl.ds(pl.multiple_of(x * 32, 32), 32)]
    zo = (1 - quad) * 4 + pos
    others = pl.ds(pl.multiple_of((1 - quad) * 4, 4), 4)

    def rows_z(piece, i, device):
        return remote(piece, piece, xz_s.at[i], xz_r.at[i], device)

    def x_quad():
        @pl.when(pos + quad < 4)
        def _():
            pl.semaphore_wait(near_in, (3 - pos) + (1 - quad))

        for o in (1, 2, 3):
            c = remote(mine, xs.at[zl, x], xz_s.at[o - 1], xz_r.at[o - 1], q_dev(o))
            c.start()
            pending.append(c)

    def x_other():
        c = remote(mine, xs.at[zl, x], xz_s.at[3], xz_r.at[3], z4_dev)
        c.start()
        pending.append(c)

    def x_pass():
        rows_z(xs.at[zo, x], 3, z4_dev).wait_recv()
        for o in (1, 2, 3):
            c = rows_z(xs.at[zo, x], 3 + o, q_dev(o))
            c.start()
            pending.append(c)

    def rows_x(hop, way, i, q, lines):
        if i < 3:
            piece = xs.at[quad * 4 + lax.rem(pos + 3 - i, 4), lax.rem(q, 4), lines]
        else:
            piece = xs.at[others, lax.rem(q, 4), lines]
        return remote(piece, piece, xx_s.at[hop, way, i], xx_r.at[hop, way, i], x_dev(3 if way else 1))

    ALL, HALF = pl.ds(0, 32), (pl.ds(0, 16), pl.ds(16, 16))

    def x_row(i):
        if i < 3:
            rows_z(xs.at[quad * 4 + lax.rem(pos + 3 - i, 4), x], i, q_dev(1)).wait_recv()
        else:
            for o in (1, 2, 3):
                rows_z(xs.at[(1 - quad) * 4 + lax.rem(pos + 4 - o, 4), x], 3 + o, q_dev(1)).wait_recv()
        for way in (0, 1):
            c = rows_x(0, way, i, x, ALL)
            c.start()
            pending.append(c)

    def x_row_pass(i):
        for way in (0, 1):
            q = x + 1 if way else x + 3
            rows_x(0, way, i, q, ALL).wait_recv()
            c = rows_x(1, way, i, q, HALF[way])
            c.start()
            pending.append(c)

    def x_row_end(i):
        for way in (0, 1):
            rows_x(1, way, i, x + 2, HALF[way]).wait_recv()

    def x_row_quad():
        for i in range(3):
            x_row(i)

    def x_row_quad_pass():
        for i in range(3):
            x_row_pass(i)

    def product(qd, t):
        rows = pl.ds(pl.multiple_of(qd * 4, 4), 4)
        cols = pl.ds(pl.multiple_of(t * 256, 256), 256)
        lhs = xs[rows, :, :, cols].reshape(512, 256)
        rhs = g[pl.ds(pl.multiple_of(qd * 2, 2), 2)].reshape(512, 1024)
        return lax.dot_general(lhs, rhs, (((0,), (0,)), ((), ())), preferred_element_type=F32)

    def weight_quad():
        for c in loads_x:
            c.wait()
        for i in range(3):
            x_row_end(i)

        @pl.loop(0, 4)
        def _(t):
            acc[pl.ds(pl.multiple_of(t * 256, 256), 256), :] = product(quad, t)

    def weight_other():
        x_row_end(3)

        @pl.loop(0, 4)
        def _(t):
            rows = pl.ds(pl.multiple_of(t * 256, 256), 256)
            dw[rows, :] = ((acc[rows, :] + product(1 - quad, t)) * (1.0 / 1024)).astype(BF16)
            pltpu.make_async_copy(dw.at[rows], dw_hbm.at[rows], out_sem.at[t]).start()

    def input_grad():
        for c in cross():
            c.wait_recv()
        mine_ph = jnp.where(quad == zh, 0, 1)
        ig_ref[...] = (fin[mine_ph] + decode(bc_r, bk_r)).astype(BF16)

    near_spread()
    near_part(0)
    far_send()
    near_part(1)
    far_take(0)
    far_take(1)
    x_quad()
    x_other()
    sum_x(0, 0)
    sum_x(0, 1)
    far_part(0)
    far_part(1)
    x_pass()
    sum_quad(0, 0, zh)
    sum_quad(0, 1, zh)
    x_row_quad()
    sum_x(1, 0)
    x_row_quad_pass()
    sum_x(1, 1)
    x_row(3)
    sum_quad(1, 0, far)
    sum_quad(1, 1, far)
    x_row_pass(3)
    weight_quad()
    input_grad()
    weight_other()

    for c in pending:
        c.wait_send()
    for c in cross():
        c.wait_send()
    for ph in (0, 1):
        for s in range(3):
            for c in to_quad(ph, s, q_dev(1)):
                c.wait_send()

    @pl.loop(0, 4)
    def _(t):
        rows = pl.ds(pl.multiple_of(t * 256, 256), 256)
        pltpu.make_async_copy(dw.at[rows], dw_hbm.at[rows], out_sem.at[t]).wait()


def per_device(inputs, out_grad, weight):
    dma = pltpu.SemaphoreType.DMA
    vmem = pltpu.VMEM
    return pl.pallas_call(
        kernel,
        out_shape=(
            jax.ShapeDtypeStruct((32, 1024), BF16),
            jax.ShapeDtypeStruct((1024, 1024), BF16),
        ),
        in_specs=[pl.BlockSpec(memory_space=pl.ANY)] * 3,
        out_specs=(pl.BlockSpec(memory_space=vmem), pl.BlockSpec(memory_space=pl.ANY)),
        scratch_shapes=[
            vmem((1024, 1024), BF16),
            vmem((4, 2, 2, 64, 1024), BF16),
            vmem((8, 4, 32, 1024), BF16),
            vmem((1024, 1024), F32),
            vmem((1024, 1024), BF16),
            vmem((256, 1024), F32),
            vmem((2, 2, 64, 1024), F32),
            vmem((2, 32, 1024), F32),
            vmem((2, 2, 3, 64, 1024), BF16),
            vmem((2, 2, 3, 64, 1024), BF16),
            vmem((2, 2, 3, 8, 128), F32),
            vmem((2, 2, 3, 8, 128), F32),
            vmem((2, 3, 32, 1024), BF16),
            vmem((2, 3, 32, 1024), BF16),
            vmem((2, 3, 8, 128), F32),
            vmem((2, 3, 8, 128), F32),
            vmem((32, 1024), BF16),
            vmem((32, 1024), BF16),
            vmem((8, 128), F32),
            vmem((8, 128), F32),
            dma((6,)),
            dma((4,)),
            pltpu.SemaphoreType.REGULAR,
            pltpu.SemaphoreType.REGULAR,
            dma((2,)),
            dma((2,)),
            dma((2, 2, 3)),
            dma((2, 2, 3)),
            dma((2, 2, 4)),
            dma((2, 2, 4)),
            dma((2, 2, 3)),
            dma((2, 2, 3)),
            dma((2, 2, 3)),
            dma((2, 2, 3)),
            dma((2, 3)),
            dma((2, 3)),
            dma((2, 3)),
            dma((2, 3)),
            dma((2,)),
            dma((2,)),
            dma((7,)),
            dma((7,)),
            dma((2, 2, 4)),
            dma((2, 2, 4)),
        ],
        compiler_params=pltpu.CompilerParams(
            collective_id=0, has_side_effects=True, vmem_limit_bytes=63 * 1024 * 1024
        ),
        cost_estimate=pl.CostEstimate(flops=4 * 1024**3, bytes_accessed=7 * 1024**2, transcendentals=0),
        name="grads",
    )(inputs, out_grad, weight)


def solution(mesh):
    return jax.shard_map(
        per_device,
        mesh=mesh,
        in_specs=(P("row", "col"), P("col", ("depth", "row")), P("col", ("depth", "row"))),
        out_specs=(P(("depth", "row"), "col"), P("col", ("depth", "row"))),
        check_vma=False,
    )
```

```python
import jax
import jax.numpy as jnp
from jax import lax
from jax.experimental import pallas as pl
from jax.experimental.pallas import tpu as pltpu
from jax.sharding import PartitionSpec as P

MESH = pl.DeviceIdType.MESH
F32 = jnp.float32
BF16 = jnp.bfloat16
PEAK = 200.0


def encode(value, code_ref, scale_ref):
    size = jnp.abs(value)
    top = jnp.max(jnp.max(size, axis=0, keepdims=True), axis=1, keepdims=True)
    top = jnp.maximum(top, 1e-30)
    power = size * (PEAK / top)
    for _ in range(4):
        power = power * power
    code_ref[...] = jnp.where(value < 0, -power, power).astype(BF16)
    scale_ref[...] = jnp.broadcast_to(top * (1.0 / PEAK), scale_ref.shape)


def decode(code_ref, scale_ref):
    code = code_ref[...].astype(F32)
    size = jnp.exp2(jnp.log2(jnp.abs(code)) * 0.0625)
    size = jnp.where(code == 0, 0.0, size) * scale_ref[0:1, 0:1]
    return jnp.where(code < 0, -size, size)


def kernel(
    x_hbm, g_hbm, w_hbm, ig_ref, dw_hbm,
    w, g, xs, acc, dw, part, own, fin,
    xc_s, xc_r, xk_s, xk_r,
    zc_s, zc_r, zk_s, zk_r,
    bc_s, bc_r, bk_s, bk_r,
    local, out_sem, near_in, far_in,
    gz_s, gz_r, gy_s, gy_r, gk_s, gk_r,
    cx_s, cx_r, kx_s, kx_r,
    cz_s, cz_r, kz_s, kz_r,
    cb_s, cb_r,
    xz_s, xz_r, xx_s, xx_r,
):
    x = lax.axis_index("depth")
    zl = lax.axis_index("row")
    col = lax.axis_index("col")
    y, zh, core = col // 4, (col // 2) % 2, col % 2
    quad, pos = zl // 4, zl % 4

    def y_dev(o):
        return (x, zl, lax.rem(y + o, 4) * 4 + zh * 2 + core)

    def x_dev(o):
        return (lax.rem(x + o, 4), zl, col)

    def q_dev(o):
        return (x, quad * 4 + lax.rem(pos + o, 4), col)

    z8_dev = (x, zl, y * 4 + (1 - zh) * 2 + core)
    sib_dev = (x, zl, y * 4 + zh * 2 + (1 - core))
    z4_dev = (x, (1 - quad) * 4 + pos, col)

    def remote(src, dst, send, recv, device):
        return pltpu.make_async_remote_copy(
            src_ref=src, dst_ref=dst, send_sem=send, recv_sem=recv, device_id=device, device_id_type=MESH
        )

    load_w = pltpu.make_async_copy(w_hbm, w, local.at[0])
    load_g = pltpu.make_async_copy(g_hbm, g.at[y, zh, core], local.at[1])
    load_w.start()
    load_g.start()
    loads_x = []
    for q in range(4):
        c = pltpu.make_async_copy(x_hbm.at[pl.ds(q * 32, 32)], xs.at[zl, q], local.at[2 + q])
        c.start()
        loads_x.append(c)

    def signal(semaphore, device):
        pl.semaphore_signal(semaphore, inc=1, device_id=device, device_id_type=MESH)

    barrier = pltpu.get_barrier_semaphore()
    for device in [sib_dev] + [f(o) for f in (y_dev, x_dev) for o in (1, 2, 3)]:
        signal(barrier, device)
    for o in (1, 2, 3):
        pl.when(pos + o < 4)(lambda o=o: signal(barrier, q_dev(o)))
    pl.when(quad == 0)(lambda: signal(barrier, z4_dev))
    pl.when(zh == 0)(lambda: signal(barrier, z8_dev))
    pl.semaphore_wait(barrier, 7 + pos + quad + zh)
    pl.when(zh == 1)(lambda: signal(far_in, z8_dev))
    for o in (1, 2, 3):
        pl.when(pos + o >= 4)(lambda o=o: signal(near_in, q_dev(o)))
    pl.when(quad == 1)(lambda: signal(near_in, z4_dev))

    pending = []

    far = 1 - zh
    to_far = [remote(g_hbm.at[pl.ds(32 * h, 32)], g.at[y, zh, core, pl.ds(32 * h, 32)], gz_s.at[h], gz_r.at[h], z8_dev) for h in (0, 1)]
    pending += to_far

    @pl.when(zh == 1)
    def _():
        for c in to_far:
            c.start()

    def chunk(yy, zz, kk, h):
        return g.at[yy, zz, kk, pl.ds(32 * h, 32)]

    def spread(ph, h, zz):
        src = g_hbm.at[pl.ds(32 * h, 32)] if ph == 0 else chunk(y, zz, core, h)
        dst = chunk(y, zz, core, h)
        for o in (1, 3, 2):
            c = remote(src, dst, gy_s.at[ph, h, o - 1], gy_r.at[ph, h, o - 1], y_dev(o))
            c.start()
            pending.append(c)
        c = remote(src, dst, gk_s.at[ph, h, 0], gk_r.at[ph, h, 0], sib_dev)
        c.start()
        pending.append(c)

    def collect(ph, h, zz):
        for o in (1, 3, 2):
            block = chunk(lax.rem(y + 4 - o, 4), zz, core, h)
            remote(block, block, gy_s.at[ph, h, o - 1], gy_r.at[ph, h, o - 1], y_dev(o)).wait_recv()
            c = remote(block, block, gk_s.at[ph, h, o], gk_r.at[ph, h, o], sib_dev)
            c.start()
            pending.append(c)
        for o in (0, 1, 3, 2):
            block = chunk(lax.rem(y + 4 - o, 4), zz, 1 - core, h)
            remote(block, block, gk_s.at[ph, h, o], gk_r.at[ph, h, o], sib_dev).wait_recv()

    def partial(ph, h, zz):
        part[...] = lax.dot_general(
            g[:, zz, :, pl.ds(32 * h, 32), :].reshape(256, 1024),
            w[...],
            (((1,), (1,)), ((), ())),
            preferred_element_type=F32,
        )

        for o in (2, 1, 3):
            target = lax.rem(x + o, 4)
            rows = pl.ds(pl.multiple_of(target * 64, 64), 64)
            s = o - 1
            encode(part[rows, :], xc_s.at[ph, h, s], xk_s.at[ph, h, s])
            c = remote(xc_s.at[ph, h, s], xc_r.at[ph, h, s], cx_s.at[ph, h, s], cx_r.at[ph, h, s], x_dev(o))
            c.start()
            pending.append(c)
            c = remote(xk_s.at[ph, h, s], xk_r.at[ph, h, s], kx_s.at[ph, h, s], kx_r.at[ph, h, s], x_dev(o))
            c.start()
            pending.append(c)
        own[ph, h] = part[pl.ds(pl.multiple_of(x * 64, 64), 64), :]

    def to_quad(ph, slot, device):
        code = remote(zc_s.at[ph, slot], zc_r.at[ph, slot], cz_s.at[ph, slot], cz_r.at[ph, slot], device)
        scale = remote(zk_s.at[ph, slot], zk_r.at[ph, slot], kz_s.at[ph, slot], kz_r.at[ph, slot], device)
        return code, scale

    def sum_x(ph, h):
        for s in range(3):
            remote(xc_s.at[ph, h, s], xc_r.at[ph, h, s], cx_s.at[ph, h, s], cx_r.at[ph, h, s], x_dev(1)).wait_recv()
            remote(xk_s.at[ph, h, s], xk_r.at[ph, h, s], kx_s.at[ph, h, s], kx_r.at[ph, h, s], x_dev(1)).wait_recv()
        for k in (0, 1):
            rows = pl.ds(k * 32, 32)
            total = own[ph, h, rows, :]
            for s in range(3):
                total = total + decode(xc_r.at[ph, h, s, rows], xk_r.at[ph, h, s])
            own[ph, h, rows, :] = total
            there = 2 * k + h

            @pl.when(pos != there)
            def _():
                slot = lax.rem(there - pos + 4, 4) - 1
                encode(own[ph, h, rows, :], zc_s.at[ph, slot], zk_s.at[ph, slot])
                for c in to_quad(ph, slot, (x, quad * 4 + there, col)):
                    c.start()

    def cross():
        code = remote(bc_s, bc_r, cb_s.at[0], cb_r.at[0], z4_dev)
        scale = remote(bk_s, bk_r, cb_s.at[1], cb_r.at[1], z4_dev)
        return code, scale

    def sum_quad(ph, h, zz):
        @pl.when(lax.rem(pos, 2) == h)
        def _():
            total = own[ph, h, pl.ds(pl.multiple_of(pos // 2 * 32, 32), 32), :]
            for s in range(3):
                for c in to_quad(ph, s, q_dev(1)):
                    c.wait_recv()
                total = total + decode(zc_r.at[ph, s], zk_r.at[ph, s])
            fin[ph] = total

            @pl.when(zz != quad)
            def _():
                encode(fin[ph], bc_s, bk_s)
                for c in cross():
                    c.start()

    def near_spread():
        for h in (0, 1):
            spread(0, h, zh)
        load_g.wait()
        load_w.wait()

    def near_part(h):
        collect(0, h, zh)
        partial(0, h, zh)

    def far_send():
        @pl.when(zh == 0)
        def _():
            pl.semaphore_wait(far_in, 1)
            for c in to_far:
                c.start()

    def far_take(h):
        block = chunk(y, far, core, h)
        remote(block, block, gz_s.at[h], gz_r.at[h], z8_dev).wait_recv()
        spread(1, h, far)

    def far_part(h):
        collect(1, h, far)
        partial(1, h, far)

    mine = x_hbm.at[pl.ds(pl.multiple_of(x * 32, 32), 32)]
    zo = (1 - quad) * 4 + pos
    others = pl.ds(pl.multiple_of((1 - quad) * 4, 4), 4)

    def rows_z(piece, i, device):
        return remote(piece, piece, xz_s.at[i], xz_r.at[i], device)

    def x_quad():
        @pl.when(pos + quad < 4)
        def _():
            pl.semaphore_wait(near_in, (3 - pos) + (1 - quad))

        for o in (1, 2, 3):
            c = remote(mine, xs.at[zl, x], xz_s.at[o - 1], xz_r.at[o - 1], q_dev(o))
            c.start()
            pending.append(c)

    def x_other():
        c = remote(mine, xs.at[zl, x], xz_s.at[3], xz_r.at[3], z4_dev)
        c.start()
        pending.append(c)

    def x_pass():
        rows_z(xs.at[zo, x], 3, z4_dev).wait_recv()
        for o in (1, 2, 3):
            c = rows_z(xs.at[zo, x], 3 + o, q_dev(o))
            c.start()
            pending.append(c)

    def rows_x(hop, way, i, q, lines):
        if i < 3:
            piece = xs.at[quad * 4 + lax.rem(pos + 3 - i, 4), lax.rem(q, 4), lines]
        else:
            piece = xs.at[others, lax.rem(q, 4), lines]
        return remote(piece, piece, xx_s.at[hop, way, i], xx_r.at[hop, way, i], x_dev(3 if way else 1))

    ALL, HALF = pl.ds(0, 32), (pl.ds(0, 16), pl.ds(16, 16))

    def x_row(i):
        if i < 3:
            rows_z(xs.at[quad * 4 + lax.rem(pos + 3 - i, 4), x], i, q_dev(1)).wait_recv()
        else:
            for o in (1, 2, 3):
                rows_z(xs.at[(1 - quad) * 4 + lax.rem(pos + 4 - o, 4), x], 3 + o, q_dev(1)).wait_recv()
        for way in (0, 1):
            c = rows_x(0, way, i, x, ALL)
            c.start()
            pending.append(c)

    def x_row_pass(i):
        for way in (0, 1):
            q = x + 1 if way else x + 3
            rows_x(0, way, i, q, ALL).wait_recv()
            c = rows_x(1, way, i, q, HALF[way])
            c.start()
            pending.append(c)

    def x_row_end(i):
        for way in (0, 1):
            rows_x(1, way, i, x + 2, HALF[way]).wait_recv()

    def x_row_quad():
        for i in range(3):
            x_row(i)

    def x_row_quad_pass():
        for i in range(3):
            x_row_pass(i)

    def product(qd, t):
        rows = pl.ds(pl.multiple_of(qd * 4, 4), 4)
        cols = pl.ds(pl.multiple_of(t * 256, 256), 256)
        lhs = xs[rows, :, :, cols].reshape(512, 256)
        rhs = g[pl.ds(pl.multiple_of(qd * 2, 2), 2)].reshape(512, 1024)
        return lax.dot_general(lhs, rhs, (((0,), (0,)), ((), ())), preferred_element_type=F32)

    def weight_quad():
        for c in loads_x:
            c.wait()
        for i in range(3):
            x_row_end(i)

        @pl.loop(0, 4)
        def _(t):
            acc[pl.ds(pl.multiple_of(t * 256, 256), 256), :] = product(quad, t)

    def weight_other():
        x_row_end(3)

        @pl.loop(0, 4)
        def _(t):
            rows = pl.ds(pl.multiple_of(t * 256, 256), 256)
            dw[rows, :] = ((acc[rows, :] + product(1 - quad, t)) * (1.0 / 1024)).astype(BF16)
            pltpu.make_async_copy(dw.at[rows], dw_hbm.at[rows], out_sem.at[t]).start()

    def input_grad():
        for c in cross():
            c.wait_recv()
        mine_ph = jnp.where(quad == zh, 0, 1)
        ig_ref[...] = (fin[mine_ph] + decode(bc_r, bk_r)).astype(BF16)

    near_spread()
    x_quad()
    near_part(0)
    far_send()
    near_part(1)
    far_take(0)
    far_take(1)
    x_other()
    x_row_quad()
    sum_x(0, 0)
    sum_x(0, 1)
    far_part(0)
    far_part(1)
    x_pass()
    x_row_quad_pass()
    sum_quad(0, 0, zh)
    sum_quad(0, 1, zh)
    sum_x(1, 0)
    sum_x(1, 1)
    x_row(3)
    sum_quad(1, 0, far)
    sum_quad(1, 1, far)
    x_row_pass(3)
    weight_quad()
    input_grad()
    weight_other()

    for c in pending:
        c.wait_send()
    for c in cross():
        c.wait_send()
    for ph in (0, 1):
        for s in range(3):
            for c in to_quad(ph, s, q_dev(1)):
                c.wait_send()

    @pl.loop(0, 4)
    def _(t):
        rows = pl.ds(pl.multiple_of(t * 256, 256), 256)
        pltpu.make_async_copy(dw.at[rows], dw_hbm.at[rows], out_sem.at[t]).wait()


def per_device(inputs, out_grad, weight):
    dma = pltpu.SemaphoreType.DMA
    vmem = pltpu.VMEM
    return pl.pallas_call(
        kernel,
        out_shape=(
            jax.ShapeDtypeStruct((32, 1024), BF16),
            jax.ShapeDtypeStruct((1024, 1024), BF16),
        ),
        in_specs=[pl.BlockSpec(memory_space=pl.ANY)] * 3,
        out_specs=(pl.BlockSpec(memory_space=vmem), pl.BlockSpec(memory_space=pl.ANY)),
        scratch_shapes=[
            vmem((1024, 1024), BF16),
            vmem((4, 2, 2, 64, 1024), BF16),
            vmem((8, 4, 32, 1024), BF16),
            vmem((1024, 1024), F32),
            vmem((1024, 1024), BF16),
            vmem((256, 1024), F32),
            vmem((2, 2, 64, 1024), F32),
            vmem((2, 32, 1024), F32),
            vmem((2, 2, 3, 64, 1024), BF16),
            vmem((2, 2, 3, 64, 1024), BF16),
            vmem((2, 2, 3, 8, 128), F32),
            vmem((2, 2, 3, 8, 128), F32),
            vmem((2, 3, 32, 1024), BF16),
            vmem((2, 3, 32, 1024), BF16),
            vmem((2, 3, 8, 128), F32),
            vmem((2, 3, 8, 128), F32),
            vmem((32, 1024), BF16),
            vmem((32, 1024), BF16),
            vmem((8, 128), F32),
            vmem((8, 128), F32),
            dma((6,)),
            dma((4,)),
            pltpu.SemaphoreType.REGULAR,
            pltpu.SemaphoreType.REGULAR,
            dma((2,)),
            dma((2,)),
            dma((2, 2, 3)),
            dma((2, 2, 3)),
            dma((2, 2, 4)),
            dma((2, 2, 4)),
            dma((2, 2, 3)),
            dma((2, 2, 3)),
            dma((2, 2, 3)),
            dma((2, 2, 3)),
            dma((2, 3)),
            dma((2, 3)),
            dma((2, 3)),
            dma((2, 3)),
            dma((2,)),
            dma((2,)),
            dma((7,)),
            dma((7,)),
            dma((2, 2, 4)),
            dma((2, 2, 4)),
        ],
        compiler_params=pltpu.CompilerParams(
            collective_id=0, has_side_effects=True, vmem_limit_bytes=63 * 1024 * 1024
        ),
        cost_estimate=pl.CostEstimate(flops=4 * 1024**3, bytes_accessed=7 * 1024**2, transcendentals=0),
        name="grads",
    )(inputs, out_grad, weight)


def solution(mesh):
    return jax.shard_map(
        per_device,
        mesh=mesh,
        in_specs=(P("row", "col"), P("col", ("depth", "row")), P("col", ("depth", "row"))),
        out_specs=(P(("depth", "row"), "col"), P("col", ("depth", "row"))),
        check_vma=False,
    )
```

```python
import jax
import jax.numpy as jnp
from jax import lax
from jax.experimental import pallas as pl
from jax.experimental.pallas import tpu as pltpu
from jax.sharding import PartitionSpec as P

MESH = pl.DeviceIdType.MESH
F32 = jnp.float32
BF16 = jnp.bfloat16
PEAK = 200.0


def encode(value, code_ref, scale_ref):
    size = jnp.abs(value)
    top = jnp.max(jnp.max(size, axis=0, keepdims=True), axis=1, keepdims=True)
    top = jnp.maximum(top, 1e-30)
    power = size * (PEAK / top)
    for _ in range(4):
        power = power * power
    code_ref[...] = jnp.where(value < 0, -power, power).astype(BF16)
    scale_ref[...] = jnp.broadcast_to(top * (1.0 / PEAK), scale_ref.shape)


def decode(code_ref, scale_ref):
    code = code_ref[...].astype(F32)
    size = jnp.exp2(jnp.log2(jnp.abs(code)) * 0.0625)
    size = jnp.where(code == 0, 0.0, size) * scale_ref[0:1, 0:1]
    return jnp.where(code < 0, -size, size)


def kernel(
    x_hbm, g_hbm, w_hbm, ig_ref, dw_hbm,
    w, g, xs, acc, dw, part, own, fin,
    xc_s, xc_r, xk_s, xk_r,
    zc_s, zc_r, zk_s, zk_r,
    bc_s, bc_r, bk_s, bk_r,
    local, out_sem, near_in, far_in,
    gz_s, gz_r, gy_s, gy_r, gk_s, gk_r,
    cx_s, cx_r, kx_s, kx_r,
    cz_s, cz_r, kz_s, kz_r,
    cb_s, cb_r,
    xz_s, xz_r, xx_s, xx_r,
):
    x = lax.axis_index("depth")
    zl = lax.axis_index("row")
    col = lax.axis_index("col")
    y, zh, core = col // 4, (col // 2) % 2, col % 2
    quad, pos = zl // 4, zl % 4

    def y_dev(o):
        return (x, zl, lax.rem(y + o, 4) * 4 + zh * 2 + core)

    def x_dev(o):
        return (lax.rem(x + o, 4), zl, col)

    def q_dev(o):
        return (x, quad * 4 + lax.rem(pos + o, 4), col)

    z8_dev = (x, zl, y * 4 + (1 - zh) * 2 + core)
    sib_dev = (x, zl, y * 4 + zh * 2 + (1 - core))
    z4_dev = (x, (1 - quad) * 4 + pos, col)

    def remote(src, dst, send, recv, device):
        return pltpu.make_async_remote_copy(
            src_ref=src, dst_ref=dst, send_sem=send, recv_sem=recv, device_id=device, device_id_type=MESH
        )

    load_w = pltpu.make_async_copy(w_hbm, w, local.at[0])
    load_g = pltpu.make_async_copy(g_hbm, g.at[y, zh, core], local.at[1])
    load_w.start()
    load_g.start()
    loads_x = []
    for q in range(4):
        c = pltpu.make_async_copy(x_hbm.at[pl.ds(q * 32, 32)], xs.at[zl, q], local.at[2 + q])
        c.start()
        loads_x.append(c)

    def signal(semaphore, device):
        pl.semaphore_signal(semaphore, inc=1, device_id=device, device_id_type=MESH)

    barrier = pltpu.get_barrier_semaphore()
    for device in [sib_dev] + [f(o) for f in (y_dev, x_dev) for o in (1, 2, 3)]:
        signal(barrier, device)
    for o in (1, 2, 3):
        pl.when(pos + o < 4)(lambda o=o: signal(barrier, q_dev(o)))
    pl.when(quad == 0)(lambda: signal(barrier, z4_dev))
    pl.when(zh == 0)(lambda: signal(barrier, z8_dev))
    pl.semaphore_wait(barrier, 7 + pos + quad + zh)
    pl.when(zh == 1)(lambda: signal(far_in, z8_dev))
    for o in (1, 2, 3):
        pl.when(pos + o >= 4)(lambda o=o: signal(near_in, q_dev(o)))
    pl.when(quad == 1)(lambda: signal(near_in, z4_dev))

    pending = []

    far = 1 - zh
    to_far = []
    for i in range(4):
        lines = pl.ds(16 * i, 16)
        to_far.append(remote(g_hbm.at[lines], g.at[y, zh, core, lines], gz_s.at[i], gz_r.at[i], z8_dev))
    pending += to_far

    @pl.when(zh == 1)
    def _():
        for c in to_far:
            c.start()

    def chunk(yy, zz, kk, h):
        return g.at[yy, zz, kk, pl.ds(32 * h, 32)]

    def spread(ph, h, zz):
        src = g_hbm.at[pl.ds(32 * h, 32)] if ph == 0 else chunk(y, zz, core, h)
        dst = chunk(y, zz, core, h)
        for o in (2, 1, 3):
            c = remote(src, dst, gy_s.at[ph, h, o - 1], gy_r.at[ph, h, o - 1], y_dev(o))
            c.start()
            pending.append(c)
        c = remote(src, dst, gk_s.at[ph, h, 0], gk_r.at[ph, h, 0], sib_dev)
        c.start()
        pending.append(c)

    def collect(ph, h, zz):
        for o in (1, 3, 2):
            block = chunk(lax.rem(y + 4 - o, 4), zz, core, h)
            remote(block, block, gy_s.at[ph, h, o - 1], gy_r.at[ph, h, o - 1], y_dev(o)).wait_recv()
            c = remote(block, block, gk_s.at[ph, h, o], gk_r.at[ph, h, o], sib_dev)
            c.start()
            pending.append(c)
        for o in (0, 1, 3, 2):
            block = chunk(lax.rem(y + 4 - o, 4), zz, 1 - core, h)
            remote(block, block, gk_s.at[ph, h, o], gk_r.at[ph, h, o], sib_dev).wait_recv()

    def partial(ph, h, zz):
        part[...] = lax.dot_general(
            g[:, zz, :, pl.ds(32 * h, 32), :].reshape(256, 1024),
            w[...],
            (((1,), (1,)), ((), ())),
            preferred_element_type=F32,
        )

        for o in (2, 1, 3):
            target = lax.rem(x + o, 4)
            rows = pl.ds(pl.multiple_of(target * 64, 64), 64)
            s = o - 1
            encode(part[rows, :], xc_s.at[ph, h, s], xk_s.at[ph, h, s])
            c = remote(xc_s.at[ph, h, s], xc_r.at[ph, h, s], cx_s.at[ph, h, s], cx_r.at[ph, h, s], x_dev(o))
            c.start()
            pending.append(c)
            c = remote(xk_s.at[ph, h, s], xk_r.at[ph, h, s], kx_s.at[ph, h, s], kx_r.at[ph, h, s], x_dev(o))
            c.start()
            pending.append(c)
        own[ph, h] = part[pl.ds(pl.multiple_of(x * 64, 64), 64), :]

    def to_quad(ph, slot, device):
        code = remote(zc_s.at[ph, slot], zc_r.at[ph, slot], cz_s.at[ph, slot], cz_r.at[ph, slot], device)
        scale = remote(zk_s.at[ph, slot], zk_r.at[ph, slot], kz_s.at[ph, slot], kz_r.at[ph, slot], device)
        return code, scale

    def sum_x(ph, h):
        for s in range(3):
            remote(xc_s.at[ph, h, s], xc_r.at[ph, h, s], cx_s.at[ph, h, s], cx_r.at[ph, h, s], x_dev(1)).wait_recv()
            remote(xk_s.at[ph, h, s], xk_r.at[ph, h, s], kx_s.at[ph, h, s], kx_r.at[ph, h, s], x_dev(1)).wait_recv()
        for k in (0, 1):
            rows = pl.ds(k * 32, 32)
            total = own[ph, h, rows, :]
            for s in range(3):
                total = total + decode(xc_r.at[ph, h, s, rows], xk_r.at[ph, h, s])
            own[ph, h, rows, :] = total
            there = 2 * k + h

            @pl.when(pos != there)
            def _():
                slot = lax.rem(there - pos + 4, 4) - 1
                encode(own[ph, h, rows, :], zc_s.at[ph, slot], zk_s.at[ph, slot])
                for c in to_quad(ph, slot, (x, quad * 4 + there, col)):
                    c.start()

    def cross():
        code = remote(bc_s, bc_r, cb_s.at[0], cb_r.at[0], z4_dev)
        scale = remote(bk_s, bk_r, cb_s.at[1], cb_r.at[1], z4_dev)
        return code, scale

    def sum_quad(ph, h, zz):
        @pl.when(lax.rem(pos, 2) == h)
        def _():
            total = own[ph, h, pl.ds(pl.multiple_of(pos // 2 * 32, 32), 32), :]
            for s in range(3):
                for c in to_quad(ph, s, q_dev(1)):
                    c.wait_recv()
                total = total + decode(zc_r.at[ph, s], zk_r.at[ph, s])
            fin[ph] = total

            @pl.when(zz != quad)
            def _():
                encode(fin[ph], bc_s, bk_s)
                for c in cross():
                    c.start()

    def near_spread():
        for h in (0, 1):
            spread(0, h, zh)
        load_g.wait()
        load_w.wait()

    def near_part(h):
        collect(0, h, zh)
        partial(0, h, zh)

    def far_send():
        @pl.when(zh == 0)
        def _():
            pl.semaphore_wait(far_in, 1)
            for c in to_far:
                c.start()

    def far_take(h):
        for i in (2 * h, 2 * h + 1):
            block = g.at[y, far, core, pl.ds(16 * i, 16)]
            remote(block, block, gz_s.at[i], gz_r.at[i], z8_dev).wait_recv()
        spread(1, h, far)

    def far_part(h):
        collect(1, h, far)
        partial(1, h, far)

    mine = x_hbm.at[pl.ds(pl.multiple_of(x * 32, 32), 32)]
    zo = (1 - quad) * 4 + pos
    others = pl.ds(pl.multiple_of((1 - quad) * 4, 4), 4)

    def rows_z(piece, i, device):
        return remote(piece, piece, xz_s.at[i], xz_r.at[i], device)

    def x_quad():
        @pl.when(pos + quad < 4)
        def _():
            pl.semaphore_wait(near_in, (3 - pos) + (1 - quad))

        for o in (1, 2, 3):
            c = remote(mine, xs.at[zl, x], xz_s.at[o - 1], xz_r.at[o - 1], q_dev(o))
            c.start()
            pending.append(c)

    def x_other():
        c = remote(mine, xs.at[zl, x], xz_s.at[3], xz_r.at[3], z4_dev)
        c.start()
        pending.append(c)

    def x_pass():
        rows_z(xs.at[zo, x], 3, z4_dev).wait_recv()
        for o in (1, 2, 3):
            c = rows_z(xs.at[zo, x], 3 + o, q_dev(o))
            c.start()
            pending.append(c)

    def rows_x(hop, way, i, q, lines):
        if i < 3:
            piece = xs.at[quad * 4 + lax.rem(pos + 3 - i, 4), lax.rem(q, 4), lines]
        else:
            piece = xs.at[others, lax.rem(q, 4), lines]
        return remote(piece, piece, xx_s.at[hop, way, i], xx_r.at[hop, way, i], x_dev(3 if way else 1))

    ALL, HALF = pl.ds(0, 32), (pl.ds(0, 16), pl.ds(16, 16))

    def x_row(i):
        if i < 3:
            rows_z(xs.at[quad * 4 + lax.rem(pos + 3 - i, 4), x], i, q_dev(1)).wait_recv()
        else:
            for o in (1, 2, 3):
                rows_z(xs.at[(1 - quad) * 4 + lax.rem(pos + 4 - o, 4), x], 3 + o, q_dev(1)).wait_recv()
        for way in (0, 1):
            c = rows_x(0, way, i, x, ALL)
            c.start()
            pending.append(c)

    def x_row_pass(i):
        for way in (0, 1):
            q = x + 1 if way else x + 3
            rows_x(0, way, i, q, ALL).wait_recv()
            c = rows_x(1, way, i, q, HALF[way])
            c.start()
            pending.append(c)

    def x_row_end(i):
        for way in (0, 1):
            rows_x(1, way, i, x + 2, HALF[way]).wait_recv()

    def x_row_quad():
        for i in range(3):
            x_row(i)

    def x_row_quad_pass():
        for i in range(3):
            x_row_pass(i)

    def product(qd, t):
        rows = pl.ds(pl.multiple_of(qd * 4, 4), 4)
        cols = pl.ds(pl.multiple_of(t * 256, 256), 256)
        lhs = xs[rows, :, :, cols].reshape(512, 256)
        rhs = g[pl.ds(pl.multiple_of(qd * 2, 2), 2)].reshape(512, 1024)
        return lax.dot_general(lhs, rhs, (((0,), (0,)), ((), ())), preferred_element_type=F32)

    def weight_quad():
        for c in loads_x:
            c.wait()
        for i in range(3):
            x_row_end(i)

        @pl.loop(0, 4)
        def _(t):
            acc[pl.ds(pl.multiple_of(t * 256, 256), 256), :] = product(quad, t)

    def weight_other():
        x_row_end(3)

        @pl.loop(0, 4)
        def _(t):
            rows = pl.ds(pl.multiple_of(t * 256, 256), 256)
            dw[rows, :] = ((acc[rows, :] + product(1 - quad, t)) * (1.0 / 1024)).astype(BF16)
            pltpu.make_async_copy(dw.at[rows], dw_hbm.at[rows], out_sem.at[t]).start()

    def input_grad():
        for c in cross():
            c.wait_recv()
        mine_ph = jnp.where(quad == zh, 0, 1)
        ig_ref[...] = (fin[mine_ph] + decode(bc_r, bk_r)).astype(BF16)

    near_spread()
    x_quad()
    near_part(0)
    far_send()
    near_part(1)
    far_take(0)
    far_take(1)
    x_other()
    x_row_quad()
    far_part(0)
    sum_x(0, 0)
    sum_x(0, 1)
    far_part(1)
    x_pass()
    x_row_quad_pass()
    sum_quad(0, 0, zh)
    sum_quad(0, 1, zh)
    sum_x(1, 0)
    sum_x(1, 1)
    x_row(3)
    weight_quad()
    sum_quad(1, 0, far)
    sum_quad(1, 1, far)
    x_row_pass(3)
    input_grad()
    weight_other()

    for c in pending:
        c.wait_send()
    for c in cross():
        c.wait_send()
    for ph in (0, 1):
        for s in range(3):
            for c in to_quad(ph, s, q_dev(1)):
                c.wait_send()

    @pl.loop(0, 4)
    def _(t):
        rows = pl.ds(pl.multiple_of(t * 256, 256), 256)
        pltpu.make_async_copy(dw.at[rows], dw_hbm.at[rows], out_sem.at[t]).wait()


def per_device(inputs, out_grad, weight):
    dma = pltpu.SemaphoreType.DMA
    vmem = pltpu.VMEM
    return pl.pallas_call(
        kernel,
        out_shape=(
            jax.ShapeDtypeStruct((32, 1024), BF16),
            jax.ShapeDtypeStruct((1024, 1024), BF16),
        ),
        in_specs=[pl.BlockSpec(memory_space=pl.ANY)] * 3,
        out_specs=(pl.BlockSpec(memory_space=vmem), pl.BlockSpec(memory_space=pl.ANY)),
        scratch_shapes=[
            vmem((1024, 1024), BF16),
            vmem((4, 2, 2, 64, 1024), BF16),
            vmem((8, 4, 32, 1024), BF16),
            vmem((1024, 1024), F32),
            vmem((1024, 1024), BF16),
            vmem((256, 1024), F32),
            vmem((2, 2, 64, 1024), F32),
            vmem((2, 32, 1024), F32),
            vmem((2, 2, 3, 64, 1024), BF16),
            vmem((2, 2, 3, 64, 1024), BF16),
            vmem((2, 2, 3, 8, 128), F32),
            vmem((2, 2, 3, 8, 128), F32),
            vmem((2, 3, 32, 1024), BF16),
            vmem((2, 3, 32, 1024), BF16),
            vmem((2, 3, 8, 128), F32),
            vmem((2, 3, 8, 128), F32),
            vmem((32, 1024), BF16),
            vmem((32, 1024), BF16),
            vmem((8, 128), F32),
            vmem((8, 128), F32),
            dma((6,)),
            dma((4,)),
            pltpu.SemaphoreType.REGULAR,
            pltpu.SemaphoreType.REGULAR,
            dma((4,)),
            dma((4,)),
            dma((2, 2, 3)),
            dma((2, 2, 3)),
            dma((2, 2, 4)),
            dma((2, 2, 4)),
            dma((2, 2, 3)),
            dma((2, 2, 3)),
            dma((2, 2, 3)),
            dma((2, 2, 3)),
            dma((2, 3)),
            dma((2, 3)),
            dma((2, 3)),
            dma((2, 3)),
            dma((2,)),
            dma((2,)),
            dma((7,)),
            dma((7,)),
            dma((2, 2, 4)),
            dma((2, 2, 4)),
        ],
        compiler_params=pltpu.CompilerParams(
            collective_id=0, has_side_effects=True, vmem_limit_bytes=63 * 1024 * 1024
        ),
        cost_estimate=pl.CostEstimate(flops=4 * 1024**3, bytes_accessed=7 * 1024**2, transcendentals=0),
        name="grads",
    )(inputs, out_grad, weight)


def solution(mesh):
    return jax.shard_map(
        per_device,
        mesh=mesh,
        in_specs=(P("row", "col"), P("col", ("depth", "row")), P("col", ("depth", "row"))),
        out_specs=(P(("depth", "row"), "col"), P("col", ("depth", "row"))),
        check_vma=False,
    )
```
